256 devices in a mesh: pair: 16 (over z, x_lo), side: 2 (over core), tp: 8 (over x_hi, y).
Axes of the slice: x: 4 (x_hi: 2, x_lo: 2; x = x_hi * 2 + x_lo), y: 4, z: 8, core: 2. Of those that a mesh axis runs over, the one named last changes fastest.
Arguments:
- token_ids: int32 [768], P(('side', 'tp')), may hold values from 0 to 76031
- embed_table: bfloat16 [76032, 8192], P(('side', 'tp'), 'pair'), may hold values from -6 to 6
- norm_gain: float32 [2, 8192], P(None, 'pair'), may hold values from 0.25 to 1.75
- w_gate: bfloat16 [2, 8192, 16384], P(None, 'pair', ('side', 'tp')), may hold values from -0.0625 to 0.0625
- w_up: bfloat16 [2, 8192, 16384], P(None, 'pair', ('side', 'tp')), may hold values from -0.0625 to 0.0625
- gate_scale: float32 [2, 16384], P(None, ('side', 'tp')), may hold values from 0.5 to 2
- up_scale: float32 [2, 16384], P(None, ('side', 'tp')), may hold values from 0.5 to 2
- w_down: bfloat16 [2, 16384, 8192], P(None, ('side', 'tp'), 'pair'), may hold values from -0.046875 to 0.046875
- down_scale: float32 [2, 8192], P(None, 'pair'), may hold values from 0.5 to 2
Outputs:
- hidden: bfloat16 [768, 8192], P(('side', 'tp'), 'pair')
The draws below stay inside these ranges and needn't reach their ends.
All inputs are finite; a program needn't handle non-finite values.
Results may differ from the reference program's by a relative error of at most 0.039.
Values may be sent and summed in bfloat16 or wider, within the bound.
No kernel may reach another device: no remote copies, remote signals or barrier semaphores. Data moves between devices by JAX's collectives and lax.ppermute only.
A program may use at most 64 MiB of HBM per device.

```python
import math
import jax
import jax.numpy as jnp
import numpy as np
from jax import lax

D = 8192
FF = 16384
VOCAB = 76032
LAYERS = 2
TOKENS = 768
N_PAIR = 16


def plant(result, rng, low, top_value):
    longest = result.shape.index(max(result.shape))
    spots = []
    for shift in (0, 1):
        where = [jax.random.randint(jax.random.fold_in(rng, axis), (), 0, length) for axis, length in enumerate(result.shape)]
        where[longest] = (where[longest] + shift) % result.shape[longest]
        spots.append(tuple(where))
    return result.at[spots[0]].set(low).at[spots[1]].set(top_value)


def steps_of(own_key, extent, split, smallest, top_value):
    level, own = 1.0, jax.random.fold_in(own_key, 6)
    for axis_at, blocks in split:
        heights = jnp.exp(jax.random.uniform(jax.random.fold_in(own, axis_at), (blocks,), jnp.float32, smallest / len(split), top_value / len(split)))
        level = level * jnp.repeat(heights, extent[axis_at] // blocks).reshape([-1 if axis == axis_at else 1 for axis in range(len(extent))])
    return level


def ranked_wide(own_key, extent, count, skew):
    loads = [min(1 << octave, count + 1 - (1 << octave)) * (1 << 20) // math.isqrt((1 << octave) ** skew) + 1 for octave in range((count + 1).bit_length()) if 1 << octave <= count]
    spread = 1 + sum(loads) // (1 << 30)
    table = np.cumsum(np.array([max(1, weight // spread) for weight in loads]))
    lot = jax.random.randint(jax.random.fold_in(own_key, 1), extent, 0, int(table[len(loads) - 1]))
    start = jnp.left_shift(1, jnp.searchsorted(jnp.asarray(table, jnp.int32), lot, side="right").astype(jnp.int32))
    grade = start - 1 + jax.random.randint(jax.random.fold_in(own_key, 4), extent, 0, 1 << 30) % jnp.minimum(start, count + 1 - start)
    return jax.random.permutation(jax.random.fold_in(own_key, 2), count)[grade].astype(jnp.int32)


def scatter_about(own_key, dims, scale, reach, shards=(), held_as=jnp.bfloat16):
    factor_of = steps_of(own_key, dims, shards, -0.22, 0.18) if shards else 1.0
    result = jax.random.normal(own_key, dims, jnp.float32) * scale * factor_of
    return jnp.minimum(jnp.maximum(result, -reach), reach).astype(held_as)


def setup_inputs(seed: int = 0) -> dict:
    key_of = jax.random.split(jax.random.key(seed), 10)
    token_ids = plant(ranked_wide(key_of[0], (TOKENS,), VOCAB, 2), jax.random.fold_in(key_of[0], 3), 0, VOCAB - 1).astype(jnp.int32)
    embed_table = scatter_about(key_of[1], (VOCAB, D), 1.0, 6.0, ((0, 16), (1, 16)))
    norm_gain = jnp.clip(1.0 + 0.15 * jax.random.normal(key_of[2], (LAYERS, D), jnp.float32), 0.25, 1.75)
    w_gate = scatter_about(key_of[3], (LAYERS, D, FF), D ** -0.5, 0.0625, ((1, 16), (2, 16)))
    w_up = scatter_about(key_of[4], (LAYERS, D, FF), D ** -0.5, 0.0625, ((1, 16), (2, 16)))
    gate_scale = jnp.clip(jnp.exp(math.log(2.0) - 1.3862944 * jax.random.uniform(key_of[5], (LAYERS, FF), jnp.float32) ** steps_of(key_of[5], (LAYERS, FF), ((1, 16),), -0.2, 0.2)), 0.5, 2.0)
    up_scale = jnp.clip(jnp.exp(math.log(2.0) - 1.3862944 * jax.random.uniform(key_of[6], (LAYERS, FF), jnp.float32) ** steps_of(key_of[6], (LAYERS, FF), ((1, 16),), -0.2, 0.2)), 0.5, 2.0)
    w_down = scatter_about(key_of[7], (LAYERS, FF, D), FF ** -0.5, 0.046875, ((1, 16), (2, 16)))
    down_scale = jnp.clip(jnp.exp(math.log(2.0) - 1.3862944 * jax.random.uniform(key_of[8], (LAYERS, D), jnp.float32) ** steps_of(key_of[8], (LAYERS, D), ((1, 16),), -0.2, 0.2)), 0.5, 2.0)
    return dict(token_ids=token_ids, embed_table=embed_table, norm_gain=norm_gain, w_gate=w_gate, w_up=w_up, gate_scale=gate_scale, up_scale=up_scale, w_down=w_down, down_scale=down_scale)


def rebf(value):
    return lax.optimization_barrier(value.astype(jnp.bfloat16)).astype(jnp.float32)

def reference(token_ids, embed_table, norm_gain, w_gate, w_up, gate_scale, up_scale, w_down, down_scale):
    x = jnp.take(embed_table, token_ids, axis=0)
    block = D // N_PAIR
    for layer in range(LAYERS):
        xf = x.astype(jnp.float32)
        mean_sq = lax.optimization_barrier(jnp.mean(xf * xf, axis=1, keepdims=True))
        normed = (xf * lax.rsqrt(mean_sq + 1e-05) * norm_gain[layer][None, :]).astype(jnp.bfloat16)
        gate_w = w_gate[layer]
        up_w = w_up[layer]

        def add_block(carry, index):
            start = (index * block).astype(jnp.int32)
            rows = lax.dynamic_slice_in_dim(normed, start, block, 1)
            gate_piece = lax.dynamic_slice_in_dim(gate_w, start, block, 0)
            up_piece = lax.dynamic_slice_in_dim(up_w, start, block, 0)
            gate_part = rebf(jnp.dot(rows, gate_piece, preferred_element_type=jnp.float32))
            up_part = rebf(jnp.dot(rows, up_piece, preferred_element_type=jnp.float32))
            return ((carry[0] + gate_part, carry[1] + up_part), None)
        zeros = jnp.zeros((TOKENS, FF), jnp.float32)
        (gate_sum, up_sum), _ = lax.scan(add_block, (zeros, zeros), jnp.arange(N_PAIR, dtype=jnp.int32))
        gate = gate_sum * gate_scale[layer][None, :]
        up = up_sum * up_scale[layer][None, :]
        act = (jax.nn.silu(gate) * up).astype(jnp.bfloat16)
        update = jnp.dot(act, w_down[layer], preferred_element_type=jnp.float32) * down_scale[layer][None, :]
        x = (xf + update).astype(jnp.bfloat16)
    return x
```

```python
import jax
import jax.numpy as jnp
from jax import lax
from jax.sharding import Mesh, PartitionSpec as P

LAYERS = 2
BF, F32 = jnp.bfloat16, jnp.float32
AXES = ("z", "xl", "c", "xh", "y")
SIZES = (8, 2, 2, 2, 4)
Z = SIZES[0]
PLANE = ("xl", "xh", "y")
OWNERS = ("c", "xh", "y")


def turn(n, by):
    return [(i, (i + by) % n) for i in range(n)]


def swap(value, axis):
    return lax.ppermute(value, axis, turn(2, 1))


def add(*terms):
    return sum(t.astype(F32) for t in terms)


def scatter_sum_z(parts):
    z = lax.axis_index("z")

    def block(offset):
        return lax.dynamic_index_in_dim(parts, lax.rem(z + offset + Z, Z), 0, keepdims=False)

    down = lax.ppermute(block(-4), "z", turn(Z, -1))
    up = None
    for far in (3, 2, 1):
        down = add(down, block(-far)).astype(BF)
        up = block(far) if up is None else add(up, block(far)).astype(BF)
        down = lax.ppermute(down, "z", turn(Z, -1))
        up = lax.ppermute(up, "z", turn(Z, 1))
    return add(down, up, block(0))


def gather_plane(x):
    n = SIZES[1] * SIZES[3] * SIZES[4]
    sent = jnp.broadcast_to(x[None], (n, *x.shape))
    got = lax.all_to_all(sent, PLANE, 0, 0, tiled=True)
    return got.reshape(SIZES[1], -1, x.shape[1])


def two_halves(value, axis, mine):
    half = value.shape[axis] // 2
    return (
        lax.dynamic_slice_in_dim(value, mine * half, half, axis),
        lax.dynamic_slice_in_dim(value, (1 - mine) * half, half, axis),
    )


def spread_weights(gate, up, down, xl):
    g_mine, g_other = two_halves(gate, 1, xl)
    u_mine, u_other = two_halves(up, 1, xl)
    gu_mine = jnp.concatenate([g_mine, u_mine], axis=1)
    gu_got = swap(jnp.concatenate([g_other, u_other], axis=1), "xl")
    first = xl == 0
    gu = jnp.concatenate([jnp.where(first, gu_mine, gu_got), jnp.where(first, gu_got, gu_mine)], axis=0)
    d_mine, d_other = two_halves(down, 0, xl)
    d_got = swap(d_other, "xl")
    d = jnp.concatenate([jnp.where(first, d_mine, d_got), jnp.where(first, d_got, d_mine)], axis=1)
    gu_sib = swap(gu, "c")
    d_sib = swap(d, "c")
    return (gu, gu_sib), (d, d_sib)


def per_device(
    token_ids, embed_table, norm_gain, w_gate, w_up, gate_scale, up_scale, w_down, down_scale
):
    xl = lax.axis_index("xl")
    owner = lax.axis_index(OWNERS)
    width = norm_gain.shape[1]
    width_total = width * SIZES[0] * SIZES[1]
    rows = token_ids.shape[0]
    own_tokens = rows * SIZES[3] * SIZES[4]

    n_owners = SIZES[2] * SIZES[3] * SIZES[4]
    all_ids = lax.all_to_all(
        jnp.broadcast_to(token_ids[None], (n_owners, rows)), OWNERS, 0, 0, tiled=True
    ).reshape(-1)
    vocab_rows = embed_table.shape[0]
    local_ids = all_ids - owner * vocab_rows
    inside = (local_ids >= 0) & (local_ids < vocab_rows)
    picked = jnp.take(embed_table, jnp.clip(local_ids, 0, vocab_rows - 1), axis=0)
    picked = jnp.where(inside[:, None], picked, jnp.zeros((), BF))

    spread = [None] * LAYERS
    spread[0] = spread_weights(w_gate[0], w_up[0], w_down[0], xl)
    gain_got = swap(norm_gain, "xl")
    gains = jnp.where(
        xl == 0, jnp.stack([norm_gain, gain_got], 1), jnp.stack([gain_got, norm_gain], 1)
    )
    scales = jnp.stack([two_halves(gate_scale, 1, xl)[0], two_halves(up_scale, 1, xl)[0]], 1)
    scales = jnp.stack([scales, swap(scales, "c")], 1)

    pieces = lax.all_to_all(picked, OWNERS, 0, 0, tiled=True).reshape(n_owners, rows, width)
    x = jnp.sum(pieces.astype(F32), axis=0).astype(BF)

    for layer in range(LAYERS):
        everyone = gather_plane(x)
        if layer + 1 < LAYERS:
            later = (w_gate[layer + 1], w_up[layer + 1], w_down[layer + 1], everyone)
            *later, everyone = lax.optimization_barrier(later)
            spread[layer + 1] = spread_weights(*later, xl)
        (gu, gu_sib), (d, d_sib) = spread[layer]
        ef = everyone.astype(F32)
        normed = (ef * gains[layer][:, None, :]).astype(BF)
        normed = jnp.concatenate([normed[0], normed[1]], axis=1)
        squares = jnp.sum((ef * ef).reshape(2, own_tokens, -1, 128), axis=(0, 2))
        parts = jnp.concatenate(
            [
                jnp.dot(normed, gu, preferred_element_type=F32).astype(BF),
                jnp.dot(normed, gu_sib, preferred_element_type=F32).astype(BF),
                squares.astype(BF),
            ],
            axis=1,
        )
        summed = scatter_sum_z(parts.reshape(Z, own_tokens // Z, -1))
        units = gu.shape[1] // 2
        inverse = lax.rsqrt(
            jnp.sum(summed[:, 4 * units :], axis=1, keepdims=True) / width_total + 1e-05
        )
        act = []
        for core in range(2):
            at = 2 * core * units
            gate = summed[:, at : at + units] * inverse * scales[layer, core, 0][None, :]
            up = summed[:, at + units : at + 2 * units] * inverse * scales[layer, core, 1][None, :]
            act.append((jax.nn.silu(gate) * up).astype(BF))
        act = lax.all_gather(jnp.concatenate(act, axis=1), "z", axis=0, tiled=True)
        weights = jnp.concatenate([d, d_sib], axis=0)
        terms = jnp.dot(act, weights, preferred_element_type=F32).astype(BF)
        terms = jnp.concatenate([terms[:, :width], terms[:, width:]], axis=0)
        got = lax.all_to_all(terms, PLANE, 0, 0, tiled=True).reshape(-1, rows, width)
        update = jnp.sum(got.astype(F32), axis=0)
        x = (x.astype(F32) + update * down_scale[layer][None, :]).astype(BF)
    return x


def solution(mesh):
    cut = Mesh(mesh.devices.reshape(SIZES), AXES)
    pair, owners = ("z", "xl"), OWNERS
    in_specs = (
        P(owners),
        P(owners, pair),
        P(None, pair),
        P(None, pair, owners),
        P(None, pair, owners),
        P(None, owners),
        P(None, owners),
        P(None, owners, pair),
        P(None, pair),
    )
    return jax.shard_map(
        per_device, mesh=cut, in_specs=in_specs, out_specs=P(owners, pair), check_vma=False
    )
```

```python
import functools

import jax
import jax.numpy as jnp
from jax import lax
from jax.experimental import pallas as pl
from jax.experimental.pallas import tpu as pltpu
from jax.sharding import Mesh, PartitionSpec as P

LAYERS = 2
BF, F32 = jnp.bfloat16, jnp.float32
AXES = ("z", "xl", "c", "xh", "y")
SIZES = (8, 2, 2, 2, 4)
Z = SIZES[0]
PLANE = ("xl", "xh", "y")
OWNERS = ("c", "xh", "y")
N_PLANE = 16
SMALL, LARGE = 18 * 2**20, 57 * 2**20

HBM = pl.BlockSpec(memory_space=pltpu.HBM)
SMEM = pl.BlockSpec(memory_space=pltpu.SMEM)
VMEM = pl.BlockSpec(memory_space=pltpu.VMEM)


def turn(n, by):
    return [(i, (i + by) % n) for i in range(n)]


def swap(value, axis):
    return lax.ppermute(value, axis, turn(2, 1))


def add(*terms):
    return sum(t.astype(F32) for t in terms)


def call(kernel, out_shape, in_specs, out_specs, scratch=(), flops=0, moved=0, vmem=LARGE):
    return pl.pallas_call(
        kernel,
        out_shape=out_shape,
        in_specs=in_specs,
        out_specs=out_specs,
        scratch_shapes=list(scratch),
        compiler_params=pltpu.CompilerParams(vmem_limit_bytes=vmem),
        cost_estimate=pl.CostEstimate(flops=flops, bytes_accessed=moved, transcendentals=0),
    )


def pack_kernel(layer, xl_ref, gate, up, down, mine, *refs):
    *others, held, in_sems, out_sems = refs
    xl = xl_ref[0]
    half = held.shape[2]
    coming, going = [], []
    for side, which in enumerate((1 - xl, xl)):
        units = pl.ds(pl.multiple_of(which * half, half), half)
        for slot, source in enumerate(
            (gate.at[layer, :, units], up.at[layer, :, units], down.at[layer, units, :])
        ):
            n = 3 * side + slot
            copy = pltpu.make_async_copy(source, held.at[n], in_sems.at[n])
            copy.start()
            coming.append(copy)
            target = mine.at[:, pl.ds(slot * half, half)] if side else others[slot]
            going.append(pltpu.make_async_copy(held.at[n], target, out_sems.at[n]))
    for come, go in zip(coming, going):
        come.wait()
        go.start()
    for go in going:
        go.wait()


def pack(layer, xl, gate, up, down):
    _, rows, cols = gate.shape
    half = cols // 2
    return call(
        functools.partial(pack_kernel, layer),
        tuple(jax.ShapeDtypeStruct((rows, n * half), BF) for n in (3, 1, 1, 1)),
        [SMEM, HBM, HBM, HBM],
        (HBM,) * 4,
        [
            pltpu.VMEM((6, rows, half), BF),
            pltpu.SemaphoreType.DMA((6,)),
            pltpu.SemaphoreType.DMA((6,)),
        ],
        moved=24 * rows * half,
    )(xl, gate, up, down)


def flat(value):
    return value.astype(F32).reshape(-1, value.shape[-1])


def store_blocks(out, value, lanes):
    rows = out.shape[1]
    for i in range(out.shape[0]):
        out[i, :, lanes] = value[i * rows : (i + 1) * rows].astype(BF)


def fetch(layout, held, sems):
    copies = []
    for n, (source, at, (slot, row, column), width) in enumerate(layout):
        target = held.at[slot, pl.ds(row, source.shape[0]), pl.ds(column, width)]
        copy = pltpu.make_async_copy(source.at[:, pl.ds(at, width)], target, sems.at[n])
        copy.start()
        copies.append(copy)
    return copies


def gate_up_kernel(layer, at_ref, x, gains, mine, gate, up, mine_sib, gate_sib, up_sib, out, lead, held, sems):
    xl, far = at_ref[0], at_ref[1]
    width = x.shape[3]
    half = held.shape[2]
    layout = []
    for core, (own, *others) in enumerate(((mine, gate, up), (mine_sib, gate_sib, up_sib))):
        for kind, other in enumerate(others):
            slot = 2 * core + kind
            layout += [(own, kind * half, (slot, 0, 0), half), (other, 0, (slot, width, 0), half)]
    copies = fetch(layout, held, sems)
    squares = 0.0
    normed = []
    for place in range(2):
        value = flat(x[xl if place == 0 else 1 - xl])
        for lane in range(0, width, 128):
            part = value[:, lane : lane + 128]
            squares = squares + part * part
        normed.append((value * gains[layer, place][None, :]).astype(BF))
    store_blocks(out, squares, slice(4 * half, 4 * half + 128))
    both = jnp.concatenate(normed, axis=1)
    for slot in range(4):
        for copy in copies[2 * slot : 2 * slot + 2]:
            copy.wait()
        total = jnp.dot(both, held[slot], preferred_element_type=F32)
        store_blocks(out, total, slice(slot * half, (slot + 1) * half))
    lead[...] = out[far]


def gate_up(layer, at, x, gains, weights):
    _, blocks, rows, width = x.shape
    half = weights[1].shape[1]
    tokens = blocks * rows
    out = jax.ShapeDtypeStruct((blocks, rows, 4 * half + 128), BF)
    return call(
        functools.partial(gate_up_kernel, layer),
        (out, jax.ShapeDtypeStruct(out.shape[1:], BF)),
        [SMEM, VMEM, VMEM] + [HBM] * 6,
        (VMEM, VMEM),
        [pltpu.VMEM((4, 2 * width, half), BF), pltpu.SemaphoreType.DMA((8,))],
        flops=16 * tokens * width * half,
        moved=2 * (8 * width * half + 2 * tokens * width + 4 * tokens * half),
        vmem=SMALL,
    )(at, x, gains, *weights)


def act_kernel(layer, width_total, a, b, c, scales, out):
    units = scales.shape[3]

    def summed(at, n):
        return add(*[t[:, at : at + n] for t in (a, b, c)])

    squares = jnp.sum(summed(4 * units, 128), axis=1, keepdims=True)
    inverse = lax.rsqrt(squares / width_total + 1e-05)
    for core in range(2):
        gate, up = (
            summed((2 * core + kind) * units, units) * inverse * scales[layer, core, kind][None, :]
            for kind in range(2)
        )
        value = (gate / (1.0 + jnp.exp(-gate)) * up).astype(BF)
        for i in range(Z):
            out[i, :, core * units : (core + 1) * units] = value


def activate(layer, width_total, terms, scales):
    rows, cols = terms[0].shape
    units = scales.shape[3]
    return call(
        functools.partial(act_kernel, layer, width_total),
        jax.ShapeDtypeStruct((Z, rows, 2 * units), BF),
        [VMEM] * 4,
        VMEM,
        flops=20 * rows * units,
        moved=8 * rows * cols,
        vmem=SMALL,
    )(*terms, scales)


def down_kernel(xl_ref, act, mine, got, mine_sib, got_sib, out, held, rows_held, made, sems):
    xl = xl_ref[0]
    units = act.shape[2] // 2
    width = held.shape[2]
    coming = pltpu.make_async_copy(act, rows_held, sems.at[4])
    coming.start()
    layout = [
        (mine, 2 * units, (0, 0, 0), width),
        (mine_sib, 2 * units, (0, units, 0), width),
        (got, 0, (1, 0, 0), width),
        (got_sib, 0, (1, units, 0), width),
    ]
    copies = fetch(layout, held, sems)
    coming.wait()
    value = rows_held[...].reshape(-1, act.shape[2])
    going = []
    for place in range(2):
        copies[2 * place].wait()
        copies[2 * place + 1].wait()
        total = jnp.dot(value, held[place], preferred_element_type=F32)
        store_blocks(made.at[place], total, slice(0, width))
        target = out.at[xl if place == 0 else 1 - xl]
        go = pltpu.make_async_copy(made.at[place], target, sems.at[5 + place])
        go.start()
        going.append(go)
    for go in going:
        go.wait()


def project(xl, act, weights):
    blocks, rows, cols = act.shape
    units, width = cols // 2, weights[1].shape[1]
    tokens = blocks * rows
    out = jax.ShapeDtypeStruct((2, blocks, rows, width), BF)
    return call(
        down_kernel,
        out,
        [SMEM] + [HBM] * 5,
        HBM,
        [
            pltpu.VMEM((2, 2 * units, width), BF),
            pltpu.VMEM(act.shape, BF),
            pltpu.VMEM(out.shape, BF),
            pltpu.SemaphoreType.DMA((7,)),
        ],
        flops=8 * tokens * units * width,
        moved=2 * (4 * units * width + 4 * tokens * width),
    )(xl, act, *weights)


def update_kernel(layer, pieces, x, scale, out, sent):
    total = add(*[pieces[i] for i in range(pieces.shape[0])])
    value = (x[...].astype(F32) + total * scale[layer][None, :]).astype(BF)
    out[...] = value
    if sent is not None:
        for i in range(sent.shape[0]):
            sent[i] = value


def first_kernel(a, b, out, sent):
    value = add(a[...], b[...]).astype(BF)
    out[...] = value
    for i in range(sent.shape[0]):
        sent[i] = value


def first(a, b):
    one = jax.ShapeDtypeStruct(a.shape, BF)
    many = jax.ShapeDtypeStruct((N_PLANE, *a.shape), BF)
    return call(first_kernel, (one, many), [VMEM] * 2, (VMEM, VMEM), moved=2 * many.size)(a, b)


def half_kernel(xh_ref, pieces, kept, given):
    xh = xh_ref[0]
    for which, out in ((xh, kept), (1 - xh, given)):
        out[...] = add(*[pieces[i, which] for i in range(pieces.shape[0])]).astype(BF)


def sum_half(xh, pieces):
    one = jax.ShapeDtypeStruct(pieces.shape[2:], BF)
    return call(half_kernel, (one, one), [SMEM, VMEM], (VMEM, VMEM), moved=2 * pieces.size)(xh, pieces)


def last_kernel(layer, pieces, x, scale, out):
    update_kernel(layer, pieces, x, scale, out, None)


def update(layer, pieces, x, scale):
    _, rows, width = pieces.shape
    one = jax.ShapeDtypeStruct((rows, width), BF)
    many = jax.ShapeDtypeStruct((N_PLANE, rows, width), BF)
    moved = 2 * pieces.size * 2
    if layer == LAYERS - 1:
        kernel = functools.partial(last_kernel, layer)
        return call(kernel, one, [VMEM] * 3, VMEM, moved=moved)(pieces, x, scale), None
    kernel = functools.partial(update_kernel, layer)
    return call(kernel, (one, many), [VMEM] * 3, (VMEM, VMEM), moved=moved)(pieces, x, scale)


def exchange(value, axes):
    return lax.all_to_all(value, axes, 0, 0, tiled=True)


def after(first, *then):
    *then, _ = lax.optimization_barrier((*then, first))
    return then if len(then) > 1 else then[0]


def together(*values):
    return lax.optimization_barrier(values)


def scatter_sum_z(parts, lead, z):
    def block(offset):
        return lax.dynamic_index_in_dim(parts, lax.rem(z + offset + Z, Z), 0, keepdims=False)

    down = lax.ppermute(lead, "z", turn(Z, -1))
    up = None
    for far in (3, 2, 1):
        down = add(down, block(-far)).astype(BF)
        up = block(far) if up is None else add(up, block(far)).astype(BF)
        down = lax.ppermute(down, "z", turn(Z, -1))
        up = lax.ppermute(up, "z", turn(Z, 1))
    return down, up, block(0)


def per_device(
    token_ids, embed_table, norm_gain, w_gate, w_up, gate_scale, up_scale, w_down, down_scale
):
    z, xl, core, xh = (lax.axis_index(axis) for axis in ("z", "xl", "c", "xh"))
    xl_arg = xl.astype(jnp.int32).reshape(1)
    xh_arg = xh.astype(jnp.int32).reshape(1)
    at_arg = jnp.stack([xl, lax.rem(z + Z // 2, Z)]).astype(jnp.int32)
    owner = lax.axis_index(OWNERS)
    width = norm_gain.shape[1]
    width_total = width * SIZES[0] * SIZES[1]
    rows = token_ids.shape[0]
    units = w_gate.shape[2] // 2
    n_owners = SIZES[2] * SIZES[3] * SIZES[4]

    all_ids = exchange(jnp.broadcast_to(token_ids[None], (n_owners, rows)), OWNERS)
    gains = jnp.stack([norm_gain, swap(norm_gain, "xl")], 1)
    scales = lax.dynamic_slice_in_dim(jnp.stack([gate_scale, up_scale], 1), xl * units, units, 2)
    scales = jnp.stack([scales, swap(scales, "c")], 1)

    mine, other = [None] * LAYERS, [None] * LAYERS
    mine[0], *other[0] = pack(0, xl_arg, w_gate, w_up, w_down)
    mine_sib = [swap(mine[0], "c"), None]
    got = [[None] * 3 for _ in range(LAYERS)]
    sib = [[None] * 3 for _ in range(LAYERS)]
    got[0][0] = swap(other[0][0], "xl")

    vocab_rows = embed_table.shape[0]
    local_ids = all_ids - owner * vocab_rows
    local_ids = local_ids.reshape(*SIZES[2:], rows).transpose(0, 2, 1, 3).reshape(-1)
    inside = (local_ids >= 0) & (local_ids < vocab_rows)
    local_ids = jnp.clip(local_ids, 0, vocab_rows - 1)
    picked = embed_table.at[local_ids].get(mode="promise_in_bounds")
    picked = jnp.where(inside[:, None], picked, jnp.zeros((), BF))
    picked, got[0][0], other[0][1], mine_sib[0], gains = together(
        picked, got[0][0], other[0][1], mine_sib[0], gains
    )
    got[0][1] = swap(other[0][1], "xl")
    pieces = exchange(picked.reshape(-1, rows, width), ("c", "y"))
    pieces = pieces.reshape(-1, SIZES[3], rows, width)
    mine[1], *other[1] = pack(1, xl_arg, *after(got[0][0], w_gate, w_up, w_down))
    pieces, got[0][1], mine[1], *other[1] = together(pieces, got[0][1], mine[1], *other[1])
    kept, given = sum_half(xh_arg, pieces)
    x, sent = first(kept, swap(given, "xh"))
    sib[0][0] = swap(got[0][0], "c")
    sib[0][1] = swap(got[0][1], "c")
    mine_sib[1] = swap(after(x, mine[1]), "c")

    for layer in range(LAYERS):
        everyone = exchange(sent, PLANE).reshape(2, -1, rows, width)
        weights = (mine[layer], *got[layer][:2], mine_sib[layer], *sib[layer][:2])
        parts, lead = gate_up(layer, at_arg, everyone, gains, weights)
        lead, other[layer][2] = together(lead, other[layer][2])
        got[layer][2] = swap(other[layer][2], "xl")
        terms = scatter_sum_z(parts, lead, z)
        act = activate(layer, width_total, terms, scales)
        if layer == 0:
            act, got[0][2], other[1][0], other[1][1] = together(
                act, got[0][2], other[1][0], other[1][1]
            )
            sib[0][2] = swap(got[0][2], "c")
            got[1][:2] = [swap(other[1][n], "xl") for n in range(2)]
        else:
            act, got[1][2] = together(act, got[1][2])
            sib[1][2] = swap(got[1][2], "c")
        act = exchange(act, "z")
        if layer == 0:
            act, got[1][0], got[1][1] = together(act, got[1][0], got[1][1])
            sib[1][:2] = [swap(got[1][n], "c") for n in range(2)]
        weights = (mine[layer], got[layer][2], mine_sib[layer], sib[layer][2])
        terms = project(xl_arg, act, weights)
        pieces = exchange(terms.reshape(N_PLANE, rows, width), PLANE)
        x, sent = update(layer, pieces, x, down_scale)
    return x


def solution(mesh):
    cut = Mesh(mesh.devices.reshape(SIZES), AXES)
    pair, owners = ("z", "xl"), OWNERS
    in_specs = (
        P(owners),
        P(owners, pair),
        P(None, pair),
        P(None, pair, owners),
        P(None, pair, owners),
        P(None, owners),
        P(None, owners),
        P(None, owners, pair),
        P(None, pair),
    )
    return jax.shard_map(
        per_device, mesh=cut, in_specs=in_specs, out_specs=P(owners, pair), check_vma=False
    )
```

```python
import functools

import jax
import jax.numpy as jnp
from jax import lax
from jax.experimental import pallas as pl
from jax.experimental.pallas import tpu as pltpu
from jax.sharding import Mesh, PartitionSpec as P

LAYERS = 2
BF, F32 = jnp.bfloat16, jnp.float32
AXES = ("z", "xl", "c", "xh", "y")
SIZES = (8, 2, 2, 2, 4)
Z = SIZES[0]
PLANE = ("xl", "xh", "y")
OWNERS = ("c", "xh", "y")
N_PLANE = 16
SMALL, LARGE = 18 * 2**20, 57 * 2**20

HBM = pl.BlockSpec(memory_space=pltpu.HBM)
SMEM = pl.BlockSpec(memory_space=pltpu.SMEM)
VMEM = pl.BlockSpec(memory_space=pltpu.VMEM)


def turn(n, by):
    return [(i, (i + by) % n) for i in range(n)]


def swap(value, axis):
    return lax.ppermute(value, axis, turn(2, 1))


def add(*terms):
    return sum(t.astype(F32) for t in terms)


def call(kernel, out_shape, in_specs, out_specs, scratch=(), flops=0, moved=0, vmem=LARGE):
    return pl.pallas_call(
        kernel,
        out_shape=out_shape,
        in_specs=in_specs,
        out_specs=out_specs,
        scratch_shapes=list(scratch),
        compiler_params=pltpu.CompilerParams(vmem_limit_bytes=vmem),
        cost_estimate=pl.CostEstimate(flops=flops, bytes_accessed=moved, transcendentals=0),
    )


def pack_kernel(layer, xl_ref, gate, up, down, mine, *refs):
    *others, held, in_sems, out_sems = refs
    xl = xl_ref[0]
    half = held.shape[2]
    coming, going = [], []
    for side, which in enumerate((1 - xl, xl)):
        units = pl.ds(pl.multiple_of(which * half, half), half)
        for slot, source in enumerate(
            (gate.at[layer, :, units], up.at[layer, :, units], down.at[layer, units, :])
        ):
            n = 3 * side + slot
            copy = pltpu.make_async_copy(source, held.at[n], in_sems.at[n])
            copy.start()
            coming.append(copy)
            if side:
                target = mine.at[:, pl.ds(slot * half, half)]
            elif len(others) == 2 and slot < 2:
                target = others[0].at[:, pl.ds(slot * half, half)]
            else:
                target = others[slot - 3]
            going.append(pltpu.make_async_copy(held.at[n], target, out_sems.at[n]))
    for come, go in zip(coming, going):
        come.wait()
        go.start()
    for go in going:
        go.wait()


def pack(layer, xl, gate, up, down, joined):
    _, rows, cols = gate.shape
    half = cols // 2
    widths = (3, 2, 1) if joined else (3, 1, 1, 1)
    return call(
        functools.partial(pack_kernel, layer),
        tuple(jax.ShapeDtypeStruct((rows, n * half), BF) for n in widths),
        [SMEM, HBM, HBM, HBM],
        (HBM,) * len(widths),
        [
            pltpu.VMEM((6, rows, half), BF),
            pltpu.SemaphoreType.DMA((6,)),
            pltpu.SemaphoreType.DMA((6,)),
        ],
        moved=24 * rows * half,
    )(xl, gate, up, down)


def flat(value):
    return value.astype(F32).reshape(-1, value.shape[-1])


def store_blocks(out, value, lanes):
    rows = out.shape[1]
    for i in range(out.shape[0]):
        out[i, :, lanes] = value[i * rows : (i + 1) * rows].astype(BF)


def fetch(layout, held, sems):
    copies = []
    for n, (source, at, (slot, row, column), width) in enumerate(layout):
        target = held.at[slot, pl.ds(row, source.shape[0]), pl.ds(column, width)]
        copy = pltpu.make_async_copy(source.at[:, pl.ds(at, width)], target, sems.at[n])
        copy.start()
        copies.append(copy)
    return copies


def gate_up_kernel(layer, at_ref, x, gains, *refs):
    *weights, out, lead, held, sems = refs
    xl, far = at_ref[0], at_ref[1]
    width = x.shape[3]
    half = held.shape[2]
    layout = []
    for core in range(2):
        own, *others = weights[core * len(weights) // 2 : (core + 1) * len(weights) // 2]
        for kind in range(2):
            slot = 2 * core + kind
            other, at = (others[kind], 0) if len(others) == 2 else (others[0], kind * half)
            layout += [(own, kind * half, (slot, 0, 0), half), (other, at, (slot, width, 0), half)]
    copies = fetch(layout, held, sems)
    squares = 0.0
    normed = []
    for place in range(2):
        value = flat(x[xl if place == 0 else 1 - xl])
        for lane in range(0, width, 128):
            part = value[:, lane : lane + 128]
            squares = squares + part * part
        normed.append((value * gains[layer, place][None, :]).astype(BF))
    store_blocks(out, squares, slice(4 * half, 4 * half + 128))
    both = jnp.concatenate(normed, axis=1)
    for slot in range(4):
        for copy in copies[2 * slot : 2 * slot + 2]:
            copy.wait()
        total = jnp.dot(both, held[slot], preferred_element_type=F32)
        store_blocks(out, total, slice(slot * half, (slot + 1) * half))
    lead[...] = out[far]


def gate_up(layer, at, x, gains, weights):
    _, blocks, rows, width = x.shape
    half = weights[0].shape[1] // 3
    tokens = blocks * rows
    out = jax.ShapeDtypeStruct((blocks, rows, 4 * half + 128), BF)
    return call(
        functools.partial(gate_up_kernel, layer),
        (out, jax.ShapeDtypeStruct(out.shape[1:], BF)),
        [SMEM, VMEM, VMEM] + [HBM] * len(weights),
        (VMEM, VMEM),
        [pltpu.VMEM((4, 2 * width, half), BF), pltpu.SemaphoreType.DMA((8,))],
        flops=16 * tokens * width * half,
        moved=2 * (8 * width * half + 2 * tokens * width + 4 * tokens * half),
        vmem=SMALL,
    )(at, x, gains, *weights)


def act_kernel(layer, width_total, a, b, c, scales, out):
    units = scales.shape[3]

    def summed(at, n):
        return add(*[t[:, at : at + n] for t in (a, b, c)])

    squares = jnp.sum(summed(4 * units, 128), axis=1, keepdims=True)
    inverse = lax.rsqrt(squares / width_total + 1e-05)
    for core in range(2):
        gate, up = (
            summed((2 * core + kind) * units, units) * inverse * scales[layer, core, kind][None, :]
            for kind in range(2)
        )
        value = (gate / (1.0 + jnp.exp(-gate)) * up).astype(BF)
        for i in range(Z):
            out[i, :, core * units : (core + 1) * units] = value


def activate(layer, width_total, terms, scales):
    rows, cols = terms[0].shape
    units = scales.shape[3]
    return call(
        functools.partial(act_kernel, layer, width_total),
        jax.ShapeDtypeStruct((Z, rows, 2 * units), BF),
        [VMEM] * 4,
        VMEM,
        flops=20 * rows * units,
        moved=8 * rows * cols,
        vmem=SMALL,
    )(*terms, scales)


def down_kernel(xl_ref, act, mine, got, mine_sib, got_sib, out, held, rows_held, made, sems):
    xl = xl_ref[0]
    units = act.shape[2] // 2
    width = held.shape[2]
    coming = pltpu.make_async_copy(act, rows_held, sems.at[4])
    coming.start()
    layout = [
        (mine, 2 * units, (0, 0, 0), width),
        (mine_sib, 2 * units, (0, units, 0), width),
        (got, 0, (1, 0, 0), width),
        (got_sib, 0, (1, units, 0), width),
    ]
    copies = fetch(layout, held, sems)
    coming.wait()
    value = rows_held[...].reshape(-1, act.shape[2])
    going = []
    for place in range(2):
        copies[2 * place].wait()
        copies[2 * place + 1].wait()
        total = jnp.dot(value, held[place], preferred_element_type=F32)
        store_blocks(made.at[place], total, slice(0, width))
        target = out.at[xl if place == 0 else 1 - xl]
        go = pltpu.make_async_copy(made.at[place], target, sems.at[5 + place])
        go.start()
        going.append(go)
    for go in going:
        go.wait()


def project(xl, act, weights):
    blocks, rows, cols = act.shape
    units, width = cols // 2, weights[1].shape[1]
    tokens = blocks * rows
    out = jax.ShapeDtypeStruct((2, blocks, rows, width), BF)
    return call(
        down_kernel,
        out,
        [SMEM] + [HBM] * 5,
        HBM,
        [
            pltpu.VMEM((2, 2 * units, width), BF),
            pltpu.VMEM(act.shape, BF),
            pltpu.VMEM(out.shape, BF),
            pltpu.SemaphoreType.DMA((7,)),
        ],
        flops=8 * tokens * units * width,
        moved=2 * (4 * units * width + 4 * tokens * width),
    )(xl, act, *weights)


def update_kernel(layer, pieces, x, scale, out, sent):
    total = add(*[pieces[i] for i in range(pieces.shape[0])])
    value = (x[...].astype(F32) + total * scale[layer][None, :]).astype(BF)
    out[...] = value
    if sent is not None:
        for i in range(sent.shape[0]):
            sent[i] = value


def first_kernel(pieces, out, sent):
    value = add(*[pieces[i] for i in range(pieces.shape[0])]).astype(BF)
    out[...] = value
    for i in range(sent.shape[0]):
        sent[i] = value


def first(pieces):
    one = jax.ShapeDtypeStruct(pieces.shape[1:], BF)
    many = jax.ShapeDtypeStruct((N_PLANE, *one.shape), BF)
    return call(first_kernel, (one, many), [VMEM], (VMEM, VMEM), moved=2 * many.size)(pieces)


def last_kernel(layer, pieces, x, scale, out):
    update_kernel(layer, pieces, x, scale, out, None)


def update(layer, pieces, x, scale):
    _, rows, width = pieces.shape
    one = jax.ShapeDtypeStruct((rows, width), BF)
    many = jax.ShapeDtypeStruct((N_PLANE, rows, width), BF)
    moved = 2 * pieces.size * 2
    if layer == LAYERS - 1:
        kernel = functools.partial(last_kernel, layer)
        return call(kernel, one, [VMEM] * 3, VMEM, moved=moved)(pieces, x, scale), None
    kernel = functools.partial(update_kernel, layer)
    return call(kernel, (one, many), [VMEM] * 3, (VMEM, VMEM), moved=moved)(pieces, x, scale)


def exchange(value, axes):
    return lax.all_to_all(value, axes, 0, 0, tiled=True)


def after(first, *then):
    *then, _ = lax.optimization_barrier((*then, first))
    return then if len(then) > 1 else then[0]


def together(*values):
    return lax.optimization_barrier(values)


def scatter_sum_z(parts, lead, z):
    def block(offset):
        return lax.dynamic_index_in_dim(parts, lax.rem(z + offset + Z, Z), 0, keepdims=False)

    down = lax.ppermute(lead, "z", turn(Z, -1))
    up = None
    for far in (3, 2, 1):
        down = add(down, block(-far)).astype(BF)
        up = block(far) if up is None else add(up, block(far)).astype(BF)
        down = lax.ppermute(down, "z", turn(Z, -1))
        up = lax.ppermute(up, "z", turn(Z, 1))
    return down, up, block(0)


def per_device(
    token_ids, embed_table, norm_gain, w_gate, w_up, gate_scale, up_scale, w_down, down_scale
):
    z, xl, core, xh = (lax.axis_index(axis) for axis in ("z", "xl", "c", "xh"))
    xl_arg = xl.astype(jnp.int32).reshape(1)
    at_arg = jnp.stack([xl, lax.rem(z + Z // 2, Z)]).astype(jnp.int32)
    owner = lax.axis_index(OWNERS)
    width = norm_gain.shape[1]
    width_total = width * SIZES[0] * SIZES[1]
    rows = token_ids.shape[0]
    units = w_gate.shape[2] // 2
    n_owners = SIZES[2] * SIZES[3] * SIZES[4]

    near = jnp.stack([token_ids, swap(token_ids, "xh")])
    near = jnp.where(xh == 0, near, near[::-1])
    gains = jnp.stack([norm_gain, swap(norm_gain, "xl")], 1)
    scales = lax.dynamic_slice_in_dim(jnp.stack([gate_scale, up_scale], 1), xl * units, units, 2)
    scales = jnp.stack([scales, swap(scales, "c")], 1)

    mine, mine_sib = [None] * LAYERS, [None] * LAYERS
    mine[0], g_out, u_out, d_out = pack(0, xl_arg, w_gate, w_up, w_down, False)
    near, g_out, gains = together(near, g_out, gains)
    g_got = swap(g_out, "xl")
    all_ids = exchange(jnp.broadcast_to(near[None], (n_owners // 2, 2, rows)), ("c", "y"))
    all_ids = all_ids.reshape(2, -1, 2, rows).transpose(0, 2, 1, 3).reshape(-1)

    vocab_rows = embed_table.shape[0]
    local_ids = all_ids - owner * vocab_rows
    inside = (local_ids >= 0) & (local_ids < vocab_rows)
    local_ids = jnp.clip(local_ids, 0, vocab_rows - 1)
    local_ids, g_got = together(local_ids, g_got)
    u_got = swap(u_out, "xl")
    picked = embed_table.at[local_ids].get(mode="promise_in_bounds")
    picked = jnp.where(inside[:, None], picked, jnp.zeros((), BF)).reshape(2, -1, rows, width)
    picked, u_got = together(picked, u_got)
    kept = lax.dynamic_index_in_dim(picked, core, 0, keepdims=False)
    given = swap(lax.dynamic_index_in_dim(picked, 1 - core, 0, keepdims=False), "c")
    both = add(kept, given).astype(BF)
    both, g_got, u_got, later = together(both, g_got, u_got, mine[0])
    mine_sib[0], g_sib, u_sib = swap(later, "c"), swap(g_got, "c"), swap(u_got, "c")
    pieces = exchange(both, ("xh", "y"))
    mine[1], gu_out, last_out = pack(1, xl_arg, *after(both, w_gate, w_up, w_down), True)
    pieces, mine_sib[0], g_sib, u_sib, mine[1], gu_out, last_out = together(
        pieces, mine_sib[0], g_sib, u_sib, mine[1], gu_out, last_out
    )
    x, sent = first(pieces)
    others, others_sib = (g_got, u_got), (g_sib, u_sib)
    mine_sib[1] = swap(after(x, mine[1]), "c")

    for layer in range(LAYERS):
        everyone = exchange(sent, PLANE).reshape(2, -1, rows, width)
        weights = (mine[layer], *others, mine_sib[layer], *others_sib)
        parts, lead = gate_up(layer, at_arg, everyone, gains, weights)
        lead, begun = together(lead, d_out if layer == 0 else last_out)
        down = swap(begun, "xl")
        act = activate(layer, width_total, scatter_sum_z(parts, lead, z), scales)
        act, down, gu_out = together(act, down, gu_out)
        down_sib = swap(down, "c")
        if layer == 0:
            gu_got = swap(gu_out, "xl")
        act = exchange(act, "z")
        if layer == 0:
            act, gu_got = together(act, gu_got)
            others, others_sib = (gu_got,), (swap(gu_got, "c"),)
        terms = project(xl_arg, act, (mine[layer], down, mine_sib[layer], down_sib))
        pieces = exchange(terms.reshape(N_PLANE, rows, width), PLANE)
        x, sent = update(layer, pieces, x, down_scale)
    return x


def solution(mesh):
    cut = Mesh(mesh.devices.reshape(SIZES), AXES)
    pair, owners = ("z", "xl"), OWNERS
    in_specs = (
        P(owners),
        P(owners, pair),
        P(None, pair),
        P(None, pair, owners),
        P(None, pair, owners),
        P(None, owners),
        P(None, owners),
        P(None, owners, pair),
        P(None, pair),
    )
    return jax.shard_map(
        per_device, mesh=cut, in_specs=in_specs, out_specs=P(owners, pair), check_vma=False
    )
```

```python
import functools

import jax
import jax.numpy as jnp
from jax import lax
from jax.experimental import pallas as pl
from jax.experimental.pallas import tpu as pltpu
from jax.sharding import Mesh, PartitionSpec as P

LAYERS = 2
BF, F32 = jnp.bfloat16, jnp.float32
AXES = ("z", "xl", "c", "xh", "y")
SIZES = (8, 2, 2, 2, 4)
Z = SIZES[0]
PLANE = ("xl", "xh", "y")
OWNERS = ("c", "xh", "y")
N_PLANE = 16
SMALL, LARGE = 18 * 2**20, 57 * 2**20

HBM = pl.BlockSpec(memory_space=pltpu.HBM)
SMEM = pl.BlockSpec(memory_space=pltpu.SMEM)
VMEM = pl.BlockSpec(memory_space=pltpu.VMEM)


def turn(n, by):
    return [(i, (i + by) % n) for i in range(n)]


def swap(value, axis):
    return lax.ppermute(value, axis, turn(2, 1))


def add(*terms):
    return sum(t.astype(F32) for t in terms)


def call(kernel, out_shape, in_specs, out_specs, scratch=(), flops=0, moved=0, vmem=LARGE):
    return pl.pallas_call(
        kernel,
        out_shape=out_shape,
        in_specs=in_specs,
        out_specs=out_specs,
        scratch_shapes=list(scratch),
        compiler_params=pltpu.CompilerParams(vmem_limit_bytes=vmem),
        cost_estimate=pl.CostEstimate(flops=flops, bytes_accessed=moved, transcendentals=0),
    )


def pack_kernel(layer, plan, xl_ref, gate, up, down, *refs):
    outs, (held, in_sems, out_sems) = refs[: len(plan)], refs[len(plan) :]
    xl = xl_ref[0]
    half = held.shape[2]
    copies = []
    for out, parts in zip(outs, plan):
        for place, (stays, kind) in enumerate(parts):
            n = len(copies)
            units = pl.ds(pl.multiple_of((xl if stays else 1 - xl) * half, half), half)
            source = (gate.at[layer, :, units], up.at[layer, :, units], down.at[layer, units, :])[kind]
            target = out.at[:, pl.ds(place * half, half)]
            come = pltpu.make_async_copy(source, held.at[n], in_sems.at[n])
            come.start()
            copies.append((come, pltpu.make_async_copy(held.at[n], target, out_sems.at[n])))
    for come, go in copies:
        come.wait()
        go.start()
    for _, go in copies:
        go.wait()


def pack(layer, plan, xl, gate, up, down):
    _, rows, cols = gate.shape
    half = cols // 2
    pieces = sum(map(len, plan))
    return call(
        functools.partial(pack_kernel, layer, plan),
        tuple(jax.ShapeDtypeStruct((rows, len(parts) * half), BF) for parts in plan),
        [SMEM, HBM, HBM, HBM],
        (HBM,) * len(plan),
        [
            pltpu.VMEM((pieces, rows, half), BF),
            pltpu.SemaphoreType.DMA((pieces,)),
            pltpu.SemaphoreType.DMA((pieces,)),
        ],
        moved=4 * pieces * rows * half,
    )(xl, gate, up, down)


def join_kernel(a, b, out, held, in_sems, out_sems):
    half = held.shape[2]
    copies = []
    for n, source in enumerate((a, b)):
        come = pltpu.make_async_copy(source, held.at[n], in_sems.at[n])
        come.start()
        target = out.at[:, pl.ds(n * half, half)]
        copies.append((come, pltpu.make_async_copy(held.at[n], target, out_sems.at[n])))
    for come, go in copies:
        come.wait()
        go.start()
    for _, go in copies:
        go.wait()


def join(a, b):
    rows, half = a.shape
    return call(
        join_kernel,
        jax.ShapeDtypeStruct((rows, 2 * half), BF),
        [HBM, HBM],
        HBM,
        [
            pltpu.VMEM((2, rows, half), BF),
            pltpu.SemaphoreType.DMA((2,)),
            pltpu.SemaphoreType.DMA((2,)),
        ],
        moved=8 * rows * half,
    )(a, b)


def flat(value):
    return value.astype(F32).reshape(-1, value.shape[-1])


def store_blocks(out, value, lanes):
    rows = out.shape[1]
    for i in range(out.shape[0]):
        out[i, :, lanes] = value[i * rows : (i + 1) * rows].astype(BF)


def fetch(layout, held, sems):
    copies = []
    for n, (source, at, (slot, row, column), width) in enumerate(layout):
        target = held.at[slot, pl.ds(row, source.shape[0]), pl.ds(column, width)]
        copy = pltpu.make_async_copy(source.at[:, pl.ds(at, width)], target, sems.at[n])
        copy.start()
        copies.append(copy)
    return copies


def gate_up_kernel(layer, at_ref, x, gains, *refs):
    *weights, out, lead, held, sems = refs
    xl, far = at_ref[0], at_ref[1]
    width = x.shape[3]
    half = held.shape[2]
    layout = []
    for core in range(2):
        own, *others = weights[core * len(weights) // 2 : (core + 1) * len(weights) // 2]
        for kind in range(2):
            slot = 2 * core + kind
            other, at = (others[kind], 0) if len(others) == 2 else (others[0], kind * half)
            layout += [(own, kind * half, (slot, 0, 0), half), (other, at, (slot, width, 0), half)]
    copies = fetch(layout, held, sems)
    squares = 0.0
    normed = []
    for place in range(2):
        value = flat(x[xl if place == 0 else 1 - xl])
        for lane in range(0, width, 128):
            part = value[:, lane : lane + 128]
            squares = squares + part * part
        normed.append((value * gains[layer, place][None, :]).astype(BF))
    store_blocks(out, squares, slice(4 * half, 4 * half + 128))
    both = jnp.concatenate(normed, axis=1)
    for slot in range(4):
        for copy in copies[2 * slot : 2 * slot + 2]:
            copy.wait()
        total = jnp.dot(both, held[slot], preferred_element_type=F32)
        store_blocks(out, total, slice(slot * half, (slot + 1) * half))
    lead[...] = out[far]


def gate_up(layer, at, x, gains, weights):
    _, blocks, rows, width = x.shape
    half = weights[0].shape[1] // 3
    tokens = blocks * rows
    out = jax.ShapeDtypeStruct((blocks, rows, 4 * half + 128), BF)
    return call(
        functools.partial(gate_up_kernel, layer),
        (out, jax.ShapeDtypeStruct(out.shape[1:], BF)),
        [SMEM, VMEM, VMEM] + [HBM] * len(weights),
        (VMEM, VMEM),
        [pltpu.VMEM((4, 2 * width, half), BF), pltpu.SemaphoreType.DMA((8,))],
        flops=16 * tokens * width * half,
        moved=2 * (8 * width * half + 2 * tokens * width + 4 * tokens * half),
        vmem=SMALL,
    )(at, x, gains, *weights)


def act_kernel(layer, width_total, a, b, c, scales, out):
    units = scales.shape[3]

    def summed(at, n):
        return add(*[t[:, at : at + n] for t in (a, b, c)])

    squares = jnp.sum(summed(4 * units, 128), axis=1, keepdims=True)
    inverse = lax.rsqrt(squares / width_total + 1e-05)
    for core in range(2):
        gate, up = (
            summed((2 * core + kind) * units, units) * inverse * scales[layer, core, kind][None, :]
            for kind in range(2)
        )
        value = (gate / (1.0 + jnp.exp(-gate)) * up).astype(BF)
        for i in range(Z):
            out[i, :, core * units : (core + 1) * units] = value


def activate(layer, width_total, terms, scales):
    rows, cols = terms[0].shape
    units = scales.shape[3]
    return call(
        functools.partial(act_kernel, layer, width_total),
        jax.ShapeDtypeStruct((Z, rows, 2 * units), BF),
        [VMEM] * 4,
        VMEM,
        flops=20 * rows * units,
        moved=8 * rows * cols,
        vmem=SMALL,
    )(*terms, scales)


def down_kernel(xl_ref, act, mine, got, mine_sib, got_sib, out, held, rows_held, made, sems):
    xl = xl_ref[0]
    units = act.shape[2] // 2
    width = held.shape[2]
    coming = pltpu.make_async_copy(act, rows_held, sems.at[4])
    coming.start()
    layout = [
        (mine, 2 * units, (0, 0, 0), width),
        (mine_sib, 2 * units, (0, units, 0), width),
        (got, 0, (1, 0, 0), width),
        (got_sib, 0, (1, units, 0), width),
    ]
    copies = fetch(layout, held, sems)
    coming.wait()
    value = rows_held[...].reshape(-1, act.shape[2])
    going = []
    for place in range(2):
        copies[2 * place].wait()
        copies[2 * place + 1].wait()
        total = jnp.dot(value, held[place], preferred_element_type=F32)
        store_blocks(made.at[place], total, slice(0, width))
        target = out.at[xl if place == 0 else 1 - xl]
        go = pltpu.make_async_copy(made.at[place], target, sems.at[5 + place])
        go.start()
        going.append(go)
    for go in going:
        go.wait()


def project(xl, act, weights):
    blocks, rows, cols = act.shape
    units, width = cols // 2, weights[1].shape[1]
    tokens = blocks * rows
    out = jax.ShapeDtypeStruct((2, blocks, rows, width), BF)
    return call(
        down_kernel,
        out,
        [SMEM] + [HBM] * 5,
        HBM,
        [
            pltpu.VMEM((2, 2 * units, width), BF),
            pltpu.VMEM(act.shape, BF),
            pltpu.VMEM(out.shape, BF),
            pltpu.SemaphoreType.DMA((7,)),
        ],
        flops=8 * tokens * units * width,
        moved=2 * (4 * units * width + 4 * tokens * width),
    )(xl, act, *weights)


def update_kernel(layer, pieces, x, scale, out, sent):
    total = add(*[pieces[i] for i in range(pieces.shape[0])])
    value = (x[...].astype(F32) + total * scale[layer][None, :]).astype(BF)
    out[...] = value
    if sent is not None:
        for i in range(sent.shape[0]):
            sent[i] = value


def first_kernel(pieces, out, sent):
    value = add(*[pieces[i] for i in range(pieces.shape[0])]).astype(BF)
    out[...] = value
    for i in range(sent.shape[0]):
        sent[i] = value


def first(pieces):
    one = jax.ShapeDtypeStruct(pieces.shape[1:], BF)
    many = jax.ShapeDtypeStruct((N_PLANE, *one.shape), BF)
    return call(first_kernel, (one, many), [VMEM], (VMEM, VMEM), moved=2 * many.size)(pieces)


def last_kernel(layer, pieces, x, scale, out):
    update_kernel(layer, pieces, x, scale, out, None)


def update(layer, pieces, x, scale):
    _, rows, width = pieces.shape
    one = jax.ShapeDtypeStruct((rows, width), BF)
    many = jax.ShapeDtypeStruct((N_PLANE, rows, width), BF)
    moved = 2 * pieces.size * 2
    if layer == LAYERS - 1:
        kernel = functools.partial(last_kernel, layer)
        return call(kernel, one, [VMEM] * 3, VMEM, moved=moved)(pieces, x, scale), None
    kernel = functools.partial(update_kernel, layer)
    return call(kernel, (one, many), [VMEM] * 3, (VMEM, VMEM), moved=moved)(pieces, x, scale)


def exchange(value, axes):
    return lax.all_to_all(value, axes, 0, 0, tiled=True)


def after(first, *then):
    *then, _ = lax.optimization_barrier((*then, first))
    return then if len(then) > 1 else then[0]


def together(*values):
    return lax.optimization_barrier(values)


def scatter_sum_z(parts, lead, z):
    def block(offset):
        return lax.dynamic_index_in_dim(parts, lax.rem(z + offset + Z, Z), 0, keepdims=False)

    down = lax.ppermute(lead, "z", turn(Z, -1))
    up = None
    for far in (3, 2, 1):
        down = add(down, block(-far)).astype(BF)
        up = block(far) if up is None else add(up, block(far)).astype(BF)
        down = lax.ppermute(down, "z", turn(Z, -1))
        up = lax.ppermute(up, "z", turn(Z, 1))
    return down, up, block(0)


def per_device(
    token_ids, embed_table, norm_gain, w_gate, w_up, gate_scale, up_scale, w_down, down_scale
):
    z, xl, core, xh = (lax.axis_index(axis) for axis in ("z", "xl", "c", "xh"))
    xl_arg = xl.astype(jnp.int32).reshape(1)
    at_arg = jnp.stack([xl, lax.rem(z + Z // 2, Z)]).astype(jnp.int32)
    owner = lax.axis_index(OWNERS)
    width = norm_gain.shape[1]
    width_total = width * SIZES[0] * SIZES[1]
    rows = token_ids.shape[0]
    units = w_gate.shape[2] // 2
    n_owners = SIZES[2] * SIZES[3] * SIZES[4]

    near = jnp.stack([token_ids, swap(token_ids, "xh")])
    near = jnp.where(xh == 0, near, near[::-1])
    gains = jnp.stack([norm_gain, swap(norm_gain, "xl")], 1)
    scales = lax.dynamic_slice_in_dim(jnp.stack([gate_scale, up_scale], 1), xl * units, units, 2)
    scales = jnp.stack([scales, swap(scales, "c")], 1)

    mine, mine_sib = [None] * LAYERS, [None] * LAYERS
    g_out, u_out = pack(0, (((0, 0),), ((0, 1),)), xl_arg, w_gate, w_up, w_down)
    stay = ((1, 0), (1, 1), (1, 2))
    near, g_out, gains = together(near, g_out, gains)
    g_got = swap(g_out, "xl")
    all_ids = exchange(jnp.broadcast_to(near[None], (n_owners // 2, 2, rows)), ("c", "y"))
    all_ids = all_ids.reshape(2, -1, 2, rows).transpose(0, 2, 1, 3).reshape(-1)

    vocab_rows = embed_table.shape[0]
    local_ids = all_ids - owner * vocab_rows
    inside = (local_ids >= 0) & (local_ids < vocab_rows)
    local_ids = jnp.clip(local_ids, 0, vocab_rows - 1)
    mine[0], d_out = pack(0, (stay, ((0, 2),)), xl_arg, *after(g_out, w_gate, w_up, w_down))
    local_ids, g_got, mine[0], d_out = together(local_ids, g_got, mine[0], d_out)
    u_got = swap(u_out, "xl")
    picked = embed_table.at[local_ids].get(mode="promise_in_bounds")
    picked = jnp.where(inside[:, None], picked, jnp.zeros((), BF)).reshape(2, -1, rows, width)
    picked, u_got = together(picked, u_got)
    kept = lax.dynamic_index_in_dim(picked, core, 0, keepdims=False)
    given = swap(lax.dynamic_index_in_dim(picked, 1 - core, 0, keepdims=False), "c")
    both = add(kept, given).astype(BF)
    both, g_got, u_got, later = together(both, g_got, u_got, mine[0])
    mine_sib[0] = swap(later, "c")
    gu_got = join(g_got, u_got)
    gu_sib = swap(gu_got, "c")
    pieces = exchange(both, ("xh", "y"))
    mine[1], gu_out, last_out = pack(
        1, (stay, ((0, 0), (0, 1)), ((0, 2),)), xl_arg, *after(both, w_gate, w_up, w_down)
    )
    pieces, mine_sib[0], mine[1], gu_out, last_out = together(
        pieces, mine_sib[0], mine[1], gu_out, last_out
    )
    x, sent = first(pieces)
    sent, gu_sib = together(sent, gu_sib)
    others, others_sib = (gu_got,), (gu_sib,)
    mine_sib[1] = swap(after(x, mine[1]), "c")

    for layer in range(LAYERS):
        everyone = exchange(sent, PLANE).reshape(2, -1, rows, width)
        weights = (mine[layer], *others, mine_sib[layer], *others_sib)
        parts, lead = gate_up(layer, at_arg, everyone, gains, weights)
        lead, begun = together(lead, d_out if layer == 0 else last_out)
        down = swap(begun, "xl")
        act = activate(layer, width_total, scatter_sum_z(parts, lead, z), scales)
        act, down, gu_out = together(act, down, gu_out)
        down_sib = swap(down, "c")
        if layer == 0:
            gu_got = swap(gu_out, "xl")
        act = exchange(act, "z")
        if layer == 0:
            act, gu_got = together(act, gu_got)
            others, others_sib = (gu_got,), (swap(gu_got, "c"),)
        terms = project(xl_arg, act, (mine[layer], down, mine_sib[layer], down_sib))
        pieces = exchange(terms.reshape(N_PLANE, rows, width), PLANE)
        x, sent = update(layer, pieces, x, down_scale)
    return x


def solution(mesh):
    cut = Mesh(mesh.devices.reshape(SIZES), AXES)
    pair, owners = ("z", "xl"), OWNERS
    in_specs = (
        P(owners),
        P(owners, pair),
        P(None, pair),
        P(None, pair, owners),
        P(None, pair, owners),
        P(None, owners),
        P(None, owners),
        P(None, owners, pair),
        P(None, pair),
    )
    return jax.shard_map(
        per_device, mesh=cut, in_specs=in_specs, out_specs=P(owners, pair), check_vma=False
    )
```

```python
import functools

import jax
import jax.numpy as jnp
from jax import lax
from jax.experimental import pallas as pl
from jax.experimental.pallas import tpu as pltpu
from jax.sharding import Mesh, PartitionSpec as P

LAYERS = 2
BF, F32 = jnp.bfloat16, jnp.float32
AXES = ("z", "xl", "c", "xh", "y")
SIZES = (8, 2, 2, 2, 4)
Z = SIZES[0]
PLANE = ("xl", "xh", "y")
OWNERS = ("c", "xh", "y")
N_PLANE = 16
SMALL, LARGE = 18 * 2**20, 57 * 2**20

HBM = pl.BlockSpec(memory_space=pltpu.HBM)
SMEM = pl.BlockSpec(memory_space=pltpu.SMEM)
VMEM = pl.BlockSpec(memory_space=pltpu.VMEM)


def turn(n, by):
    return [(i, (i + by) % n) for i in range(n)]


def swap(value, axis):
    return lax.ppermute(value, axis, turn(2, 1))


def add(*terms):
    return sum(t.astype(F32) for t in terms)


def call(kernel, out_shape, in_specs, out_specs, scratch=(), flops=0, moved=0, vmem=LARGE):
    return pl.pallas_call(
        kernel,
        out_shape=out_shape,
        in_specs=in_specs,
        out_specs=out_specs,
        scratch_shapes=list(scratch),
        compiler_params=pltpu.CompilerParams(vmem_limit_bytes=vmem),
        cost_estimate=pl.CostEstimate(flops=flops, bytes_accessed=moved, transcendentals=0),
    )


def pack_kernel(layer, plan, xl_ref, gate, up, down, *refs):
    outs, (held, in_sems, out_sems) = refs[: len(plan)], refs[len(plan) :]
    xl = xl_ref[0]
    half = held.shape[2]
    copies = []
    for out, parts in zip(outs, plan):
        for place, (stays, kind) in enumerate(parts):
            n = len(copies)
            units = pl.ds(pl.multiple_of((xl if stays else 1 - xl) * half, half), half)
            source = (gate.at[layer, :, units], up.at[layer, :, units], down.at[layer, units, :])[kind]
            target = out.at[:, pl.ds(place * half, half)]
            come = pltpu.make_async_copy(source, held.at[n], in_sems.at[n])
            come.start()
            copies.append((come, pltpu.make_async_copy(held.at[n], target, out_sems.at[n])))
    for come, go in copies:
        come.wait()
        go.start()
    for _, go in copies:
        go.wait()


def pack(layer, plan, xl, gate, up, down):
    _, rows, cols = gate.shape
    half = cols // 2
    pieces = sum(map(len, plan))
    return call(
        functools.partial(pack_kernel, layer, plan),
        tuple(jax.ShapeDtypeStruct((rows, len(parts) * half), BF) for parts in plan),
        [SMEM, HBM, HBM, HBM],
        (HBM,) * len(plan),
        [
            pltpu.VMEM((pieces, rows, half), BF),
            pltpu.SemaphoreType.DMA((pieces,)),
            pltpu.SemaphoreType.DMA((pieces,)),
        ],
        moved=4 * pieces * rows * half,
    )(xl, gate, up, down)


def join_kernel(a, b, out, held, in_sems, out_sems):
    half = held.shape[2]
    copies = []
    for n, source in enumerate((a, b)):
        come = pltpu.make_async_copy(source, held.at[n], in_sems.at[n])
        come.start()
        target = out.at[:, pl.ds(n * half, half)]
        copies.append((come, pltpu.make_async_copy(held.at[n], target, out_sems.at[n])))
    for come, go in copies:
        come.wait()
        go.start()
    for _, go in copies:
        go.wait()


def join(a, b):
    rows, half = a.shape
    return call(
        join_kernel,
        jax.ShapeDtypeStruct((rows, 2 * half), BF),
        [HBM, HBM],
        HBM,
        [
            pltpu.VMEM((2, rows, half), BF),
            pltpu.SemaphoreType.DMA((2,)),
            pltpu.SemaphoreType.DMA((2,)),
        ],
        moved=8 * rows * half,
    )(a, b)


def flat(value):
    return value.astype(F32).reshape(-1, value.shape[-1])


def store_blocks(out, value, lanes):
    rows = out.shape[1]
    for i in range(out.shape[0]):
        out[i, :, lanes] = value[i * rows : (i + 1) * rows].astype(BF)


def fetch(layout, held, sems):
    copies = []
    for n, (source, at, (slot, row, column), width) in enumerate(layout):
        target = held.at[slot, pl.ds(row, source.shape[0]), pl.ds(column, width)]
        copy = pltpu.make_async_copy(source.at[:, pl.ds(at, width)], target, sems.at[n])
        copy.start()
        copies.append(copy)
    return copies


def gate_up_kernel(layer, at_ref, x, gains, *refs):
    *weights, out, lead, held, sems = refs
    xl, far = at_ref[0], at_ref[1]
    width = x.shape[3]
    half = held.shape[2]
    layout = []
    for core in range(2):
        own, *others = weights[core * len(weights) // 2 : (core + 1) * len(weights) // 2]
        for kind in range(2):
            slot = 2 * core + kind
            other, at = (others[kind], 0) if len(others) == 2 else (others[0], kind * half)
            layout += [(own, kind * half, (slot, 0, 0), half), (other, at, (slot, width, 0), half)]
    copies = fetch(layout, held, sems)
    squares = 0.0
    normed = []
    for place in range(2):
        value = flat(x[xl if place == 0 else 1 - xl])
        for lane in range(0, width, 128):
            part = value[:, lane : lane + 128]
            squares = squares + part * part
        normed.append((value * gains[layer, place][None, :]).astype(BF))
    store_blocks(out, squares, slice(4 * half, 4 * half + 128))
    both = jnp.concatenate(normed, axis=1)
    for slot in range(4):
        for copy in copies[2 * slot : 2 * slot + 2]:
            copy.wait()
        total = jnp.dot(both, held[slot], preferred_element_type=F32)
        store_blocks(out, total, slice(slot * half, (slot + 1) * half))
    lead[...] = out[far]


def gate_up(layer, at, x, gains, weights):
    _, blocks, rows, width = x.shape
    half = weights[0].shape[1] // 3
    tokens = blocks * rows
    out = jax.ShapeDtypeStruct((blocks, rows, 4 * half + 128), BF)
    return call(
        functools.partial(gate_up_kernel, layer),
        (out, jax.ShapeDtypeStruct(out.shape[1:], BF)),
        [SMEM, VMEM, VMEM] + [HBM] * len(weights),
        (VMEM, VMEM),
        [pltpu.VMEM((4, 2 * width, half), BF), pltpu.SemaphoreType.DMA((8,))],
        flops=16 * tokens * width * half,
        moved=2 * (8 * width * half + 2 * tokens * width + 4 * tokens * half),
        vmem=SMALL,
    )(at, x, gains, *weights)


def act_kernel(layer, width_total, a, b, c, scales, out):
    units = scales.shape[3]

    def summed(at, n):
        return add(*[t[:, at : at + n] for t in (a, b, c)])

    squares = jnp.sum(summed(4 * units, 128), axis=1, keepdims=True)
    inverse = lax.rsqrt(squares / width_total + 1e-05)
    for core in range(2):
        gate, up = (
            summed((2 * core + kind) * units, units) * inverse * scales[layer, core, kind][None, :]
            for kind in range(2)
        )
        value = (gate / (1.0 + jnp.exp(-gate)) * up).astype(BF)
        for i in range(Z):
            out[i, :, core * units : (core + 1) * units] = value


def activate(layer, width_total, terms, scales):
    rows, cols = terms[0].shape
    units = scales.shape[3]
    return call(
        functools.partial(act_kernel, layer, width_total),
        jax.ShapeDtypeStruct((Z, rows, 2 * units), BF),
        [VMEM] * 4,
        VMEM,
        flops=20 * rows * units,
        moved=8 * rows * cols,
        vmem=SMALL,
    )(*terms, scales)


def down_kernel(xl_ref, act, mine, got, mine_sib, got_sib, out, held, rows_held, made, sems):
    xl = xl_ref[0]
    units = act.shape[2] // 2
    width = held.shape[2]
    coming = pltpu.make_async_copy(act, rows_held, sems.at[4])
    coming.start()
    layout = [
        (mine, 2 * units, (0, 0, 0), width),
        (mine_sib, 2 * units, (0, units, 0), width),
        (got, 0, (1, 0, 0), width),
        (got_sib, 0, (1, units, 0), width),
    ]
    copies = fetch(layout, held, sems)
    coming.wait()
    value = rows_held[...].reshape(-1, act.shape[2])
    going = []
    for place in range(2):
        copies[2 * place].wait()
        copies[2 * place + 1].wait()
        total = jnp.dot(value, held[place], preferred_element_type=F32)
        store_blocks(made.at[place], total, slice(0, width))
        target = out.at[xl if place == 0 else 1 - xl]
        go = pltpu.make_async_copy(made.at[place], target, sems.at[5 + place])
        go.start()
        going.append(go)
    for go in going:
        go.wait()


def project(xl, act, weights):
    blocks, rows, cols = act.shape
    units, width = cols // 2, weights[1].shape[1]
    tokens = blocks * rows
    out = jax.ShapeDtypeStruct((2, blocks, rows, width), BF)
    return call(
        down_kernel,
        out,
        [SMEM] + [HBM] * 5,
        HBM,
        [
            pltpu.VMEM((2, 2 * units, width), BF),
            pltpu.VMEM(act.shape, BF),
            pltpu.VMEM(out.shape, BF),
            pltpu.SemaphoreType.DMA((7,)),
        ],
        flops=8 * tokens * units * width,
        moved=2 * (4 * units * width + 4 * tokens * width),
    )(xl, act, *weights)


def update_kernel(layer, pieces, x, scale, out, sent):
    total = add(*[pieces[i] for i in range(pieces.shape[0])])
    value = (x[...].astype(F32) + total * scale[layer][None, :]).astype(BF)
    out[...] = value
    if sent is not None:
        for i in range(sent.shape[0]):
            sent[i] = value


def first_kernel(pieces, out, sent):
    value = add(*[pieces[i] for i in range(pieces.shape[0])]).astype(BF)
    out[...] = value
    for i in range(sent.shape[0]):
        sent[i] = value


def first(pieces):
    one = jax.ShapeDtypeStruct(pieces.shape[1:], BF)
    many = jax.ShapeDtypeStruct((N_PLANE, *one.shape), BF)
    return call(first_kernel, (one, many), [VMEM], (VMEM, VMEM), moved=2 * many.size)(pieces)


def last_kernel(layer, pieces, x, scale, out):
    update_kernel(layer, pieces, x, scale, out, None)


def update(layer, pieces, x, scale):
    _, rows, width = pieces.shape
    one = jax.ShapeDtypeStruct((rows, width), BF)
    many = jax.ShapeDtypeStruct((N_PLANE, rows, width), BF)
    moved = 2 * pieces.size * 2
    if layer == LAYERS - 1:
        kernel = functools.partial(last_kernel, layer)
        return call(kernel, one, [VMEM] * 3, VMEM, moved=moved)(pieces, x, scale), None
    kernel = functools.partial(update_kernel, layer)
    return call(kernel, (one, many), [VMEM] * 3, (VMEM, VMEM), moved=moved)(pieces, x, scale)


def exchange(value, axes):
    return lax.all_to_all(value, axes, 0, 0, tiled=True)


def after(first, *then):
    *then, _ = lax.optimization_barrier((*then, first))
    return then if len(then) > 1 else then[0]


def together(*values):
    return lax.optimization_barrier(values)


def scatter_sum_z(parts, lead, z):
    def block(offset):
        return lax.dynamic_index_in_dim(parts, lax.rem(z + offset + Z, Z), 0, keepdims=False)

    down = lax.ppermute(lead, "z", turn(Z, -1))
    up = None
    for far in (3, 2, 1):
        down = add(down, block(-far)).astype(BF)
        up = block(far) if up is None else add(up, block(far)).astype(BF)
        down = lax.ppermute(down, "z", turn(Z, -1))
        up = lax.ppermute(up, "z", turn(Z, 1))
    return down, up, block(0)


def per_device(
    token_ids, embed_table, norm_gain, w_gate, w_up, gate_scale, up_scale, w_down, down_scale
):
    z, xl, core, xh = (lax.axis_index(axis) for axis in ("z", "xl", "c", "xh"))
    xl_arg = xl.astype(jnp.int32).reshape(1)
    at_arg = jnp.stack([xl, lax.rem(z + Z // 2, Z)]).astype(jnp.int32)
    owner = lax.axis_index(OWNERS)
    width = norm_gain.shape[1]
    width_total = width * SIZES[0] * SIZES[1]
    rows = token_ids.shape[0]
    units = w_gate.shape[2] // 2
    n_owners = SIZES[2] * SIZES[3] * SIZES[4]

    near = jnp.stack([token_ids, swap(token_ids, "xh")])
    near = jnp.where(xh == 0, near, near[::-1])
    gains = jnp.stack([norm_gain, swap(norm_gain, "xl")], 1)
    scales = lax.dynamic_slice_in_dim(jnp.stack([gate_scale, up_scale], 1), xl * units, units, 2)
    scales = jnp.stack([scales, swap(scales, "c")], 1)

    mine, mine_sib = [None] * LAYERS, [None] * LAYERS
    g_out, u_out = pack(0, (((0, 0),), ((0, 1),)), xl_arg, w_gate, w_up, w_down)
    stay = ((1, 0), (1, 1), (1, 2))
    near, g_out, gains = together(near, g_out, gains)
    g_got = swap(g_out, "xl")
    all_ids = exchange(jnp.broadcast_to(near[None], (n_owners // 2, 2, rows)), ("c", "y"))
    all_ids = all_ids.reshape(2, -1, 2, rows).transpose(0, 2, 1, 3).reshape(-1)

    vocab_rows = embed_table.shape[0]
    local_ids = all_ids - owner * vocab_rows
    inside = (local_ids >= 0) & (local_ids < vocab_rows)
    local_ids = jnp.clip(local_ids, 0, vocab_rows - 1)
    local_ids, g_got = together(local_ids, g_got)
    mine[0], d_out = pack(0, (stay, ((0, 2),)), xl_arg, *after(g_out, w_gate, w_up, w_down))
    u_got = swap(u_out, "xl")
    picked = embed_table.at[local_ids].get(mode="promise_in_bounds")
    picked = jnp.where(inside[:, None], picked, jnp.zeros((), BF)).reshape(2, -1, rows, width)
    picked, u_got = together(picked, u_got)
    kept = lax.dynamic_index_in_dim(picked, core, 0, keepdims=False)
    given = swap(lax.dynamic_index_in_dim(picked, 1 - core, 0, keepdims=False), "c")
    both = add(kept, given).astype(BF)
    both, g_got, u_got, later = together(both, g_got, u_got, mine[0])
    mine_sib[0] = swap(later, "c")
    gu_got = join(g_got, u_got)
    gu_sib = swap(gu_got, "c")
    pieces = exchange(both, ("xh", "y"))
    mine[1], gu_out, last_out = pack(
        1, (stay, ((0, 0), (0, 1)), ((0, 2),)), xl_arg, *after(both, w_gate, w_up, w_down)
    )
    pieces, mine_sib[0], gu_sib, mine[1], gu_out, last_out = together(
        pieces, mine_sib[0], gu_sib, mine[1], gu_out, last_out
    )
    x, sent = first(pieces)
    others, others_sib = (gu_got,), (gu_sib,)
    mine_sib[1] = swap(after(x, mine[1]), "c")

    for layer in range(LAYERS):
        everyone = exchange(sent, PLANE).reshape(2, -1, rows, width)
        weights = (mine[layer], *others, mine_sib[layer], *others_sib)
        parts, lead = gate_up(layer, at_arg, everyone, gains, weights)
        lead, begun = together(lead, d_out if layer == 0 else last_out)
        down = swap(begun, "xl")
        act = activate(layer, width_total, scatter_sum_z(parts, lead, z), scales)
        act, down, gu_out = together(act, down, gu_out)
        down_sib = swap(down, "c")
        if layer == 0:
            gu_got = swap(gu_out, "xl")
        act = exchange(act, "z")
        if layer == 0:
            act, gu_got = together(act, gu_got)
            others, others_sib = (gu_got,), (swap(gu_got, "c"),)
        terms = project(xl_arg, act, (mine[layer], down, mine_sib[layer], down_sib))
        pieces = exchange(terms.reshape(N_PLANE, rows, width), PLANE)
        x, sent = update(layer, pieces, x, down_scale)
    return x


def solution(mesh):
    cut = Mesh(mesh.devices.reshape(SIZES), AXES)
    pair, owners = ("z", "xl"), OWNERS
    in_specs = (
        P(owners),
        P(owners, pair),
        P(None, pair),
        P(None, pair, owners),
        P(None, pair, owners),
        P(None, owners),
        P(None, owners),
        P(None, owners, pair),
        P(None, pair),
    )
    return jax.shard_map(
        per_device, mesh=cut, in_specs=in_specs, out_specs=P(owners, pair), check_vma=False
    )
```
